32 devices in a mesh: groups: 2 (over x), lon: 16 (over z, y, core).
Axes of the slice: x: 2, y: 2, z: 4, core: 2. Of those that a mesh axis runs over, the one named last changes fastest.
Arguments:
- atmosphere: bfloat16 [16, 512, 1024], P('groups', 'lon'), parts along dimension 0, may hold values from -6 to 6
- cotangent: bfloat16 [16, 512, 1024], P('groups', 'lon'), parts along dimension 0, may hold values from -6 to 6
- ocean_state: bfloat16 [16, 512, 512], P('groups', 'lon'), parts along dimension 0, may hold values from -6 to 6
- ocean_mask: int32 [16, 512], P('groups', 'lon'), parts along dimension 0, may hold values 0 or 1
- projection: bfloat16 [1024, 3072], P('lon'), may hold values from -9 to 9
- output_weight: bfloat16 [1024, 1024], P('lon'), may hold values from -0.1875 to 0.1875
- attention_gain: float32 [1024], replicated, may hold values from 0.5 to 1.5
- surface_embed: float32 [1024], replicated, may hold values from -3 to 3
- surface_read: bfloat16 [512], replicated, may hold values from -0.25 to 0.25
- flux_weight: bfloat16 [1024, 4], replicated, may hold values from -0.1875 to 0.1875
- flux_embed: float32 [4, 512], replicated, may hold values from -3 to 3
- depthwise: float32 [7, 7, 512], replicated, may hold values from -0.875 to 0.875
- ocean_gain: float32 [512], replicated, may hold values from 0.5 to 1.5
- expand: bfloat16 [512, 2048], replicated, may hold values from -0.25 to 0.25
- contract: bfloat16 [2048, 512], replicated, may hold values from -0.125 to 0.125
- regrid_blocks: bfloat16 [16, 2, 256, 256], P('lon'), may hold values from -0.375 to 0.375
- regrid_target: int32 [16, 2], replicated, may hold values from 0 to 15, as said below
Outputs:
- atmosphere_out: bfloat16 [16, 512, 1024], P('groups', 'lon'), parts along dimension 0
- ocean_next: bfloat16 [16, 512, 512], P('groups', 'lon'), parts along dimension 0
- weight_grad: float32 [2048, 4096], P(('groups', 'lon')), parts along dimension 0
The draws below stay inside these ranges and needn't reach their ends.
There are 2 independent parts, one for each index of `groups`. The reference program is written for one: setup_inputs(seed, part) draws one part's arguments, and reference() takes and returns one part's arrays. A program takes and returns all parts, laid end to end along the dimension named above; an argument that names none is the same for every part. Nothing has to cross between parts.
Inputs may be any that keep to these rules, and one draw needn't show every extreme that they name: `regrid_target`: column 0 names every ocean tile exactly once.
All inputs are finite; a program needn't handle non-finite values. No bound on the sum of `ocean_mask` on one device may be relied on, other than what follows from the above.
Results may differ from the reference program's by a relative error of at most 0.008.
The reference program's roundings to bfloat16 on the way count: a program that leaves them out, or rounds other values in their place, can miss the bound.
Values may be sent and summed in bfloat16 or wider, within the bound.
A program may use at most 128 MiB of HBM per device.

```python
import jax
import jax.numpy as jnp
from jax import lax

D = 1024
HEAD_DIM = 32
HEADS = 32
CO = 512
FFO = 2048
FLUXES = 4
KB = 2
WIN = 8
KERNEL = 7
LAT = 8
CELLS = 256
LON = 512
N_LON = 16


def draw_regrid_target(key, part):
    first = jax.random.permutation(jax.random.fold_in(key, 11), N_LON).astype(jnp.int32)
    others = jax.random.randint(jax.random.fold_in(key, 12), (N_LON, KB - 1), 0, N_LON).astype(jnp.int32)
    return jnp.concatenate([first[:, None], others], axis=1)


def draw_atmosphere(key, part):
    values = jnp.clip(jax.random.normal(jax.random.fold_in(key, 23), (LAT, LON, D), jnp.float32), -6.0, 6.0)
    return values.astype(jnp.bfloat16)


def draw_projection(key, part):
    scale = D ** (-0.5)
    raw = jax.random.normal(jax.random.fold_in(key, 32), (D, 3 * D), jnp.float32) * scale
    raw = jnp.clip(raw, -0.1875, 0.1875)
    return raw.astype(jnp.bfloat16)


def place_ends(entries, stream_key, smallest, largest):
    extent = entries.shape
    index_at = [jax.random.randint(jax.random.fold_in(stream_key, axis), (), 0, extent[axis]) for axis in range(len(extent))]
    entries = entries.at[tuple(index_at)].set(smallest)
    longest = extent.index(max(extent))
    index_at[longest] = (index_at[longest] + 1) % extent[longest]
    return entries.at[tuple(index_at)].set(largest)


def level_of(stream_key, dims, shards, smallest, high):
    level = 1.0
    for dim, parts in shards:
        heights = jax.random.uniform(jax.random.fold_in(jax.random.fold_in(stream_key, 6), dim), (parts,), jnp.float32, smallest / len(shards), high / len(shards))
        level = level * jnp.repeat(jnp.exp(heights), dims[dim] // parts).reshape((-1,) + (1,) * (len(dims) - 1 - dim))
    return level


def normal_values(key, shape, deviation, most, split=(), held_as=jnp.bfloat16):
    level = level_of(key, shape, split, -0.22, 0.18) if split else 1.0
    result = jax.random.normal(key, shape, jnp.float32) * deviation * level
    return jnp.minimum(jnp.maximum(result, -most), most).astype(held_as)


def setup_inputs(seed: int = 0, part: int = 0) -> dict:
    arg_keys = jax.random.split(jax.random.key(seed), 18)
    own_keys = jax.random.split(jax.random.fold_in(arg_keys[17], part), 18)
    atmosphere = draw_atmosphere(jax.random.fold_in(jax.random.fold_in(arg_keys[17], part), 71), part)
    cotangent = normal_values(own_keys[1], (LAT, LON, D), 1.0, 6.0, ((1, 16),))
    ocean_state = normal_values(own_keys[2], (LAT, LON, CO), 1.0, 6.0, ((1, 16),))
    ocean_mask = place_ends((jax.random.randint(own_keys[3], (LAT, LON), 0, 4) < 3).astype(jnp.int32), jax.random.fold_in(own_keys[3], 1), 0, 1)
    projection = draw_projection(jax.random.fold_in(arg_keys[17], 71), part)
    output_weight = normal_values(arg_keys[5], (D, D), D ** -0.5, 0.1875, ((0, 16),))
    attention_gain = jnp.clip(1.0 + 0.1 * jax.random.normal(arg_keys[6], (D,), jnp.float32), 0.5, 1.5)
    surface_embed = normal_values(arg_keys[7], (D,), 0.5, 3.0, (), jnp.float32)
    surface_read = normal_values(arg_keys[8], (CO,), CO ** -0.5, 0.25)
    flux_weight = normal_values(arg_keys[9], (D, FLUXES), D ** -0.5, 0.1875)
    flux_embed = normal_values(arg_keys[10], (FLUXES, CO), FLUXES ** -0.5, 3.0, (), jnp.float32)
    depthwise = normal_values(arg_keys[11], (KERNEL, KERNEL, CO), (KERNEL * KERNEL) ** -0.5, 0.875, (), jnp.float32)
    ocean_gain = jnp.clip(1.0 + 0.1 * jax.random.normal(arg_keys[12], (CO,), jnp.float32), 0.5, 1.5)
    expand = normal_values(arg_keys[13], (CO, FFO), CO ** -0.5, 0.25)
    contract = normal_values(arg_keys[14], (FFO, CO), FFO ** -0.5, 0.125)
    regrid_blocks = normal_values(arg_keys[15], (N_LON, KB, CELLS, CELLS), CELLS ** -0.5, 0.375, ((0, 16),))
    regrid_target = draw_regrid_target(jax.random.fold_in(arg_keys[17], 71), part)
    return dict(atmosphere=atmosphere, cotangent=cotangent, ocean_state=ocean_state, ocean_mask=ocean_mask, projection=projection, output_weight=output_weight, attention_gain=attention_gain, surface_embed=surface_embed, surface_read=surface_read, flux_weight=flux_weight, flux_embed=flux_embed, depthwise=depthwise, ocean_gain=ocean_gain, expand=expand, contract=contract, regrid_blocks=regrid_blocks, regrid_target=regrid_target)


EPSILON = 1e-05
HIGHEST = lax.Precision.HIGHEST

def layer_norm(values, gain):
    center = values - lax.optimization_barrier(jnp.mean(values, axis=-1, keepdims=True))
    spread = lax.optimization_barrier(jnp.mean(center * center, axis=-1, keepdims=True))
    return center * lax.rsqrt(spread + EPSILON) * gain

def to_windows(values, window):
    height, width, depth = values.shape
    blocks = values.reshape(height // window, window, width // window, window, depth)
    return blocks.transpose(0, 2, 1, 3, 4).reshape(-1, window * window, depth)

def from_windows(values, height, width, window):
    depth = values.shape[-1]
    blocks = values.reshape(height // window, width // window, window, window, depth)
    return blocks.transpose(0, 2, 1, 3, 4).reshape(height, width, depth)

def tiles_of(grid, count):
    height, total, depth = grid.shape
    return grid.reshape(height, count, total // count, depth).transpose(1, 0, 2, 3).reshape(count, -1, depth)

def grid_of(tiles, height):
    count, cells, depth = tiles.shape
    return tiles.reshape(count, height, cells // height, depth).transpose(1, 0, 2, 3).reshape(height, -1, depth)

def split_three(packed, heads, head_size):
    windows, tokens = (packed.shape[0], packed.shape[1])
    width = heads * head_size
    query = packed[..., :width].reshape(windows, tokens, heads, head_size).astype(jnp.float32)
    keys = packed[..., width:2 * width].reshape(windows, tokens, heads, head_size).astype(jnp.float32)
    values = packed[..., 2 * width:].reshape(windows, tokens, heads, head_size).astype(jnp.float32)
    return (query, keys, values)

def attend_forward(packed, heads, head_size):
    query, keys, values = split_three(packed, heads, head_size)
    scores = jnp.einsum('wqhd,wkhd->whqk', query, keys, precision=HIGHEST) * head_size ** (-0.5)
    probs = jax.nn.softmax(scores, axis=-1)
    weights = probs.astype(jnp.bfloat16)
    mixed = jnp.einsum('whqk,wkhd->wqhd', weights.astype(jnp.float32), values, precision=HIGHEST)
    return (mixed.reshape(packed.shape[0], packed.shape[1], heads * head_size).astype(jnp.bfloat16), probs, weights)

def attend_backward(packed, probs, weights, grad_att, heads, head_size):
    query, keys, values = split_three(packed, heads, head_size)
    windows, tokens = (packed.shape[0], packed.shape[1])
    grad_heads = grad_att.reshape(windows, tokens, heads, head_size).astype(jnp.float32)
    grad_probs = jnp.einsum('wqhd,wkhd->whqk', grad_heads, values, precision=HIGHEST)
    grad_values = jnp.einsum('whqk,wqhd->wkhd', weights.astype(jnp.float32), grad_heads, precision=HIGHEST)
    inner = lax.optimization_barrier(jnp.sum(grad_probs * probs, axis=-1, keepdims=True))
    grad_scores = (probs * (grad_probs - inner) * head_size ** (-0.5)).astype(jnp.bfloat16).astype(jnp.float32)
    grad_query = jnp.einsum('whqk,wkhd->wqhd', grad_scores, keys, precision=HIGHEST)
    grad_keys = jnp.einsum('whqk,wqhd->wkhd', grad_scores, query, precision=HIGHEST)
    width = heads * head_size
    joined = jnp.concatenate([grad_query.reshape(windows, tokens, width), grad_keys.reshape(windows, tokens, width), grad_values.reshape(windows, tokens, width)], axis=-1)
    return joined.astype(jnp.bfloat16)

def depthwise_conv(padded, kernel, height, width):
    reach = kernel.shape[0]
    total = jnp.zeros((height, width, kernel.shape[2]), jnp.float32)
    for row in range(reach):
        for column in range(reach):
            total = total + padded[row:row + height, column:column + width] * kernel[row, column]
    return total

def reference(atmosphere, cotangent, ocean_state, ocean_mask, projection, output_weight, attention_gain, surface_embed, surface_read, flux_weight, flux_embed, depthwise, ocean_gain, expand, contract, regrid_blocks, regrid_target):
    shift = WIN // 2
    surface = jnp.dot(ocean_state.reshape(-1, CO), surface_read, preferred_element_type=jnp.float32).astype(jnp.bfloat16)
    surface_tiles = tiles_of(surface.reshape(LAT, LON, 1), N_LON)[..., 0]
    picked = surface_tiles[regrid_target]
    lifted = jnp.einsum('nkcd,nkd->nc', regrid_blocks.astype(jnp.float32), picked.astype(jnp.float32), precision=HIGHEST)
    lifted_grid = grid_of(lifted[..., None], LAT)[..., 0]
    state = (atmosphere.astype(jnp.float32) + lifted_grid[..., None] * surface_embed).astype(jnp.bfloat16)
    shifted = jnp.roll(state, -shift, axis=1)
    normed = layer_norm(shifted.astype(jnp.float32), attention_gain).astype(jnp.bfloat16)
    packed = jnp.dot(normed.reshape(-1, D), projection, preferred_element_type=jnp.float32).astype(jnp.bfloat16).reshape(LAT, LON, 3 * D)
    packed_windows = to_windows(packed, WIN)
    mixed, probs, weights = attend_forward(packed_windows, HEADS, HEAD_DIM)
    attended = from_windows(mixed, LAT, LON, WIN)
    change = jnp.dot(attended.reshape(-1, D), output_weight, preferred_element_type=jnp.float32).reshape(LAT, LON, D)
    updated = (shifted.astype(jnp.float32) + change).astype(jnp.bfloat16)
    atmosphere_out = jnp.roll(updated, shift, axis=1)
    flux = jnp.dot(atmosphere_out.reshape(-1, D), flux_weight, preferred_element_type=jnp.float32).astype(jnp.bfloat16).reshape(LAT, LON, FLUXES)
    flux_tiles = tiles_of(flux, N_LON)
    pieces = jnp.einsum('ncf,nkcd->nkfd', flux_tiles.astype(jnp.float32), regrid_blocks.astype(jnp.float32), precision=HIGHEST)
    routing = (regrid_target[..., None] == jnp.arange(N_LON, dtype=jnp.int32)).astype(jnp.float32)
    arrived = jnp.einsum('nkt,nkfd->tfd', routing, pieces, precision=HIGHEST)
    arrived_grid = grid_of(arrived.transpose(0, 2, 1), LAT)
    forcing = jnp.dot(arrived_grid.reshape(-1, FLUXES), flux_embed, precision=HIGHEST).reshape(LAT, LON, CO)
    forced = (ocean_state.astype(jnp.float32) + forcing).astype(jnp.bfloat16)
    reach = KERNEL // 2
    padded = jnp.pad(forced.astype(jnp.float32), ((reach, reach), (0, 0), (0, 0)))
    padded = jnp.concatenate([padded[:, LON - reach:], padded, padded[:, :reach]], axis=1)
    conv = depthwise_conv(padded, depthwise, LAT, LON)
    ocean_normed = layer_norm(conv, ocean_gain).astype(jnp.bfloat16)
    hidden = jax.nn.gelu(jnp.dot(ocean_normed.reshape(-1, CO), expand, preferred_element_type=jnp.float32)).astype(jnp.bfloat16)
    ocean_change = jnp.dot(hidden, contract, preferred_element_type=jnp.float32).reshape(LAT, LON, CO)
    ocean_next = (ocean_state.astype(jnp.float32) + ocean_mask.astype(jnp.float32)[..., None] * ocean_change).astype(jnp.bfloat16)
    grad_shifted = jnp.roll(cotangent, -shift, axis=1).reshape(-1, D)
    grad_att = jnp.dot(grad_shifted, output_weight.T, preferred_element_type=jnp.float32).astype(jnp.bfloat16).reshape(LAT, LON, D)
    grad_packed = attend_backward(packed_windows, probs, weights, to_windows(grad_att, WIN), HEADS, HEAD_DIM)
    grad_grid = from_windows(grad_packed, LAT, LON, WIN).reshape(-1, 3 * D)
    grad_project = jnp.dot(normed.reshape(-1, D).T, grad_grid, preferred_element_type=jnp.float32)
    grad_output = jnp.dot(attended.reshape(-1, D).T, grad_shifted, preferred_element_type=jnp.float32)
    weight_grad = jnp.concatenate([grad_project, grad_output], axis=1)
    return (atmosphere_out, ocean_next, weight_grad)
```

```python
import functools

import jax
import jax.numpy as jnp
from jax import lax
from jax.experimental import pallas as pl
from jax.experimental.pallas import tpu as pltpu
from jax.sharding import PartitionSpec as P

HEAD_DIM = 32
WIN = 8
KERNEL = 7
LANES = 4
PACK = 4


EPSILON = 1e-05
HIGHEST = lax.Precision.HIGHEST
MESH = pl.DeviceIdType.MESH


def from_behind(block, axis, distance):
    devices = range(lax.axis_size(axis))
    route = [((i - distance) % len(devices), i) for i in devices]
    return lax.ppermute(block, axis, route)


def extended(shard, sides, width):
    for axis, dim in sides:
        peers, length = (lax.axis_size(axis), shard.shape[dim])
        up = [(i, (i + 1) % peers) for i in range(peers)]
        down = [(j, i) for i, j in up]
        last = lax.slice_in_dim(shard, length - width, length, axis=dim)
        leading = lax.slice_in_dim(shard, 0, width, axis=dim)
        before = lax.ppermute(last, axis, up)
        after = lax.ppermute(leading, axis, down)
        shard = jnp.concatenate([before, shard, after], axis=dim)
    return shard


def layer_norm(values, gain):
    center = values - jnp.mean(values, axis=-1, keepdims=True)
    spread = jnp.mean(center * center, axis=-1, keepdims=True)
    return center * lax.rsqrt(spread + EPSILON) * gain


def to_windows(values, window):
    height, width, depth = values.shape
    blocks = values.reshape(height // window, window, width // window, window, depth)
    return blocks.transpose(0, 2, 1, 3, 4).reshape(-1, depth)


def from_windows(values, height, width, window):
    depth = values.shape[-1]
    blocks = values.reshape(height // window, width // window, window, window, depth)
    return blocks.transpose(0, 2, 1, 3, 4).reshape(height, width, depth)


def ring_place(chip, chips):
    if chips != 8:
        return chip
    return (chip % 2) * (chips - 1 - chip // 2) + (1 - chip % 2) * (chip // 2)


def ring_chip(place, chips):
    if chips != 8:
        return place
    back = place // (chips // 2)
    return (1 - back) * (2 * place) + back * (2 * (chips - 1 - place) + 1)


def meet_all(n, me):
    barrier = pltpu.get_barrier_semaphore()

    def greet(offset, carry):
        pl.semaphore_signal(
            barrier, inc=1, device_id={"lon": (me + offset) % n}, device_id_type=MESH
        )
        return carry

    lax.fori_loop(1, n, greet, 0)
    pl.semaphore_wait(barrier, n - 1)


def direct_copy(src, dst, sems, offset, peer):
    return pltpu.make_async_remote_copy(
        src_ref=src,
        dst_ref=dst,
        send_sem=sems.at[0, offset],
        recv_sem=sems.at[1, offset],
        device_id={"lon": peer},
        device_id_type=MESH,
    )


def small_gather_kernel(n, x_ref, out_ref, sems):
    me = lax.axis_index("lon")
    meet_all(n, me)

    def send(offset, carry):
        direct_copy(x_ref, out_ref.at[me], sems, offset, (me + offset) % n).start()
        return carry

    def wait(offset, carry):
        copy = direct_copy(x_ref, out_ref.at[(me + n - offset) % n], sems, offset, (me + offset) % n)
        copy.wait()
        return carry

    lax.fori_loop(1, n, send, 0)
    out_ref[me] = x_ref[...]
    lax.fori_loop(1, n, wait, 0)


def small_gather(x, n, collective_id):
    return pl.pallas_call(
        functools.partial(small_gather_kernel, n),
        out_shape=jax.ShapeDtypeStruct((n,) + x.shape, x.dtype),
        in_specs=[pl.BlockSpec(memory_space=pltpu.VMEM)],
        out_specs=pl.BlockSpec(memory_space=pltpu.VMEM),
        scratch_shapes=[pltpu.SemaphoreType.DMA((2, n))],
        compiler_params=pltpu.CompilerParams(collective_id=collective_id, has_side_effects=True),
    )(x)


def gather_weights_kernel(
    n, proj_ref, out_weight_ref, surface_ref, w_ref, s_ref, ring_sems, pair_sems, own_sems, near_sems
):
    rows, width = out_weight_ref.shape
    chips = n // 2
    me = lax.axis_index("lon")
    core = me % 2
    place = ring_place(me // 2, chips)
    sibling = me + 1 - 2 * core

    own = []
    for lane in range(LANES):
        src = proj_ref.at[:, pl.ds(lane * width, width)] if lane < LANES - 1 else out_weight_ref
        own.append(
            pltpu.make_async_copy(
                src, w_ref.at[pl.ds(me * rows, rows), pl.ds(lane * width, width)], own_sems.at[lane]
            )
        )
        own[-1].start()
    own.append(pltpu.make_async_copy(surface_ref, s_ref.at[me], own_sems.at[LANES]))
    own[-1].start()
    meet_all(n, me)

    def send_near(offset, carry):
        direct_copy(surface_ref, s_ref.at[me], near_sems, offset, (me + offset) % n).start()
        return carry

    def wait_near(offset, carry):
        direct_copy(
            surface_ref, s_ref.at[(me + n - offset) % n], near_sems, offset, (me + offset) % n
        ).wait()
        return carry

    def slot(lane, distance, half):
        owner = ring_chip((place + distance) % chips, chips) * 2 + half
        return w_ref.at[
            pl.ds(pl.multiple_of(owner * rows, rows), rows), pl.ds(lane * width, width)
        ]

    def behind(lane, step):
        return step if lane % 2 else chips - step

    def ring_copy(lane, step, distance):
        ahead = chips - 1 if lane % 2 else 1
        block = slot(lane, distance, core)
        return pltpu.make_async_remote_copy(
            src_ref=block,
            dst_ref=block,
            send_sem=ring_sems.at[0, lane, step],
            recv_sem=ring_sems.at[1, lane, step],
            device_id={"lon": ring_chip((place + ahead) % chips, chips) * 2 + core},
            device_id_type=MESH,
        )

    def pair_copy(lane, step, half):
        block = slot(lane, behind(lane, step), half)
        return pltpu.make_async_remote_copy(
            src_ref=block,
            dst_ref=block,
            send_sem=pair_sems.at[0, lane, step],
            recv_sem=pair_sems.at[1, lane, step],
            device_id={"lon": sibling},
            device_id_type=MESH,
        )

    for copy in own:
        copy.wait()
    for lane in range(LANES):
        ring_copy(lane, 0, behind(lane, 0)).start()
    lax.fori_loop(1, n, send_near, 0)
    for lane in range(LANES):
        pair_copy(lane, 0, core).start()

    def step_on(step, carry):
        for lane in range(LANES):
            ring_copy(lane, step - 1, behind(lane, step)).wait_recv()
            ring_copy(lane, step, behind(lane, step)).start()
            pair_copy(lane, step, core).start()
        return carry

    lax.fori_loop(1, chips - 1, step_on, 0)
    for lane in range(LANES):
        ring_copy(lane, chips - 2, behind(lane, chips - 1)).wait_recv()
        pair_copy(lane, chips - 1, core).start()

    def drain(step, carry):
        for lane in range(LANES):
            ring_copy(lane, step, behind(lane, step)).wait_send()
        return carry

    def drain_pair(step, carry):
        for lane in range(LANES):
            pair_copy(lane, step, core).wait_send()
            pair_copy(lane, step, 1 - core).wait_recv()
        return carry

    lax.fori_loop(1, n, wait_near, 0)
    lax.fori_loop(0, chips - 1, drain, 0)
    lax.fori_loop(0, chips, drain_pair, 0)


def gather_weights(projection, output_weight, surface, n):
    rows, width = output_weight.shape
    chips = n // 2
    anywhere = pl.BlockSpec(memory_space=pl.ANY)
    return pl.pallas_call(
        functools.partial(gather_weights_kernel, n),
        out_shape=(
            jax.ShapeDtypeStruct((n * rows, LANES * width), projection.dtype),
            jax.ShapeDtypeStruct((n,) + surface.shape, surface.dtype),
        ),
        in_specs=[anywhere] * 3,
        out_specs=(anywhere, anywhere),
        scratch_shapes=[
            pltpu.SemaphoreType.DMA((2, LANES, chips - 1)),
            pltpu.SemaphoreType.DMA((2, LANES, chips)),
            pltpu.SemaphoreType.DMA((LANES + 1,)),
            pltpu.SemaphoreType.DMA((2, n)),
        ],
        compiler_params=pltpu.CompilerParams(collective_id=0, has_side_effects=True),
    )(projection, output_weight, surface)


def attention_kernel(packed_ref, grad_ref, attended_ref, grad_packed_ref):
    tokens, model = grad_ref.shape
    lanes = PACK * HEAD_DIM
    spread = PACK * tokens
    row_head = lax.broadcasted_iota(jnp.int32, (spread, lanes), 0) // tokens
    column_head = lax.broadcasted_iota(jnp.int32, (spread, lanes), 1) // HEAD_DIM
    own_head = row_head == column_head
    head_of = lax.broadcasted_iota(jnp.int32, (tokens, lanes), 1) // HEAD_DIM
    lower = lax.broadcasted_iota(jnp.int32, (tokens, 2 * tokens), 1) < tokens

    def expand_heads(block):
        tiled = jnp.concatenate([block] * PACK, axis=0)
        return jnp.where(own_head, tiled, jnp.zeros_like(tiled))

    def collapse_heads(block):
        total = jnp.where(head_of == 0, block[:tokens], 0.0)
        for head in range(1, PACK):
            total = total + jnp.where(head_of == head, block[head * tokens : (head + 1) * tokens], 0.0)
        return total

    def per_head(values, reduce, neutral):
        parts = []
        for start in range(0, spread, 2 * tokens):
            part = values[:, start : start + 2 * tokens]
            low = reduce(jnp.where(lower, part, neutral), axis=1, keepdims=True)
            high = reduce(jnp.where(lower, neutral, part), axis=1, keepdims=True)
            parts.append(jnp.where(lower, low, high))
        return jnp.concatenate(parts, axis=1)

    def product(left, right, contract):
        return lax.dot_general(
            left, right, (contract, ((), ())), preferred_element_type=jnp.float32
        )

    last, first = ((1,), (1,)), ((0,), (0,))
    plain = ((1,), (0,))
    scale = HEAD_DIM ** (-0.5)
    for group in range(model // lanes):
        at = group * lanes
        query = packed_ref[:, at : at + lanes]
        keys = expand_heads(packed_ref[:, model + at : model + at + lanes])
        values = expand_heads(packed_ref[:, 2 * model + at : 2 * model + at + lanes])
        grad = grad_ref[:, at : at + lanes]
        scores = product(query, keys, last) * scale
        powers = jnp.exp(scores - per_head(scores, jnp.max, -jnp.inf))
        probs = powers / per_head(powers, jnp.sum, 0.0)
        weights = probs.astype(jnp.bfloat16)
        attended_ref[:, at : at + lanes] = product(weights, values, plain).astype(jnp.bfloat16)
        grad_probs = product(grad, values, last)
        grad_values = collapse_heads(product(weights, grad, first))
        inner = per_head(grad_probs * probs, jnp.sum, 0.0)
        grad_scores = (probs * (grad_probs - inner) * scale).astype(jnp.bfloat16)
        grad_query = product(grad_scores, keys, plain)
        grad_keys = collapse_heads(product(grad_scores, query, first))
        grad_packed_ref[:, at : at + lanes] = grad_query.astype(jnp.bfloat16)
        grad_packed_ref[:, model + at : model + at + lanes] = grad_keys.astype(jnp.bfloat16)
        grad_packed_ref[:, 2 * model + at : 2 * model + at + lanes] = grad_values.astype(jnp.bfloat16)


def attention(packed, grad_att):
    tokens, model = grad_att.shape
    cells = WIN * WIN
    wide = pl.BlockSpec((cells, 3 * model), lambda w: (w, 0))
    narrow = pl.BlockSpec((cells, model), lambda w: (w, 0))
    return pl.pallas_call(
        attention_kernel,
        grid=(tokens // cells,),
        out_shape=(
            jax.ShapeDtypeStruct((tokens, model), jnp.bfloat16),
            jax.ShapeDtypeStruct((tokens, 3 * model), jnp.bfloat16),
        ),
        in_specs=[wide, narrow],
        out_specs=(narrow, wide),
        compiler_params=pltpu.CompilerParams(vmem_limit_bytes=48 * 1024 * 1024),
        cost_estimate=pl.CostEstimate(
            flops=14 * tokens * cells * model * PACK,
            bytes_accessed=16 * tokens * model,
            transcendentals=tokens * cells * (model // HEAD_DIM),
        ),
    )(packed, grad_att)


def depthwise_conv(padded, kernel, height, width):
    reach = kernel.shape[0]
    total = jnp.zeros((height, width, kernel.shape[2]), jnp.float32)
    for row in range(reach):
        for column in range(reach):
            total = (
                total + padded[row : row + height, column : column + width] * kernel[row, column]
            )
    return total


def dot32(left, right):
    return jnp.dot(left, right, preferred_element_type=jnp.float32)


def largest(values):
    return jnp.max(jnp.abs(values)).astype(jnp.float32)


def reduce_ring(terms, scale, forward, devices, position):
    chips = devices // 2
    core = position % 2
    place = ring_place(position // 2, chips)
    step_by = 1 if forward else -1
    route = []
    for device in range(devices):
        ahead = ring_chip((ring_place(device // 2, chips) + step_by) % chips, chips)
        route.append((device, ahead * 2 + device % 2))

    def term(distance):
        chip = ring_chip((place + step_by * distance + 2 * chips) % chips, chips)
        return lax.dynamic_index_in_dim(terms, chip, 0, keepdims=False) * scale

    moving = term(-1).astype(jnp.float16)
    for step in range(chips - 1):
        moving = lax.ppermute(moving, "lon", route).astype(jnp.float32) + term(-2 - step)
        if step < chips - 2:
            moving = moving.astype(jnp.float16)
    return moving / scale


def per_device(
    atmosphere,
    cotangent,
    ocean_state,
    ocean_mask,
    projection,
    output_weight,
    attention_gain,
    surface_embed,
    surface_read,
    flux_weight,
    flux_embed,
    depthwise,
    ocean_gain,
    expand,
    contract,
    regrid_blocks,
    regrid_target,
):
    height, width, model = atmosphere.shape
    channels = ocean_state.shape[2]
    shift = WIN // 2
    tokens = height * width
    devices = lax.axis_size("lon")
    position = lax.axis_index("lon")
    chips = devices // 2
    core = position % 2
    blocks = regrid_blocks[0]
    targets = lax.dynamic_index_in_dim(regrid_target, position, 0, keepdims=False)
    surface = dot32(ocean_state.reshape(tokens, channels), surface_read).astype(jnp.bfloat16)
    all_weights, surfaces = gather_weights(
        projection,
        output_weight,
        jnp.broadcast_to(surface.astype(jnp.float32)[None], (8, tokens)),
        devices,
    )
    picked = jnp.take(surfaces[:, 0], targets, axis=0).astype(jnp.bfloat16)
    lifted = jnp.einsum("kcd,kd->c", blocks, picked, preferred_element_type=jnp.float32)
    state = (
        atmosphere.astype(jnp.float32) + lifted.reshape(height, width)[..., None] * surface_embed
    ).astype(jnp.bfloat16)
    full_projection, full_output = all_weights[:, : 3 * model], all_weights[:, 3 * model :]
    edges = (
        from_behind(state[:, :shift], "lon", -1),
        from_behind(cotangent[:, :shift], "lon", -1),
    )
    shifted = to_windows(jnp.concatenate([state[:, shift:], edges[0]], axis=1), WIN)
    grad_flat = to_windows(jnp.concatenate([cotangent[:, shift:], edges[1]], axis=1), WIN)
    normed = layer_norm(shifted.astype(jnp.float32), attention_gain).astype(jnp.bfloat16)
    packed = dot32(normed, full_projection).astype(jnp.bfloat16)
    grad_att = lax.dot_general(
        grad_flat, full_output, (((1,), (1,)), ((), ())), preferred_element_type=jnp.float32
    ).astype(jnp.bfloat16)
    attended, grad_packed = attention(packed, grad_att)

    bound = tokens * jnp.maximum(
        largest(normed) * largest(grad_packed), largest(attended) * largest(grad_flat)
    )
    bounds = small_gather(jnp.full((8, 128), bound, jnp.float32), devices, 1)
    scale = 30000.0 / jnp.maximum(jnp.sum(bounds[:, 0, 0]), 1e-30)

    pairs = [(i, i + 1 - 2 * (i % 2)) for i in range(devices)]

    def split_rows(values):
        turned = values.T.reshape(chips, 2, model // devices, tokens)
        mine = lax.dynamic_index_in_dim(turned, core, 1, keepdims=False)
        other = lax.dynamic_index_in_dim(turned, 1 - core, 1, keepdims=False)
        mine, other = (part.reshape(model // 2, tokens) for part in (mine, other))
        return mine, lax.ppermute(other, "lon", pairs)

    normed_rows = split_rows(normed)
    attended_rows = split_rows(attended)
    rights = [grad_packed[:, i * model : (i + 1) * model] for i in range(3)] + [grad_flat]
    reduced = []
    for lane, right in enumerate(rights):
        rows = normed_rows if lane < 3 else attended_rows
        far = lax.ppermute(right, "lon", pairs)
        terms = (dot32(rows[0], right) + dot32(rows[1], far)).reshape(chips, -1, model)
        reduced.append(reduce_ring(terms, scale, lane % 2 == 0, devices, position))
    weight_grad = jnp.concatenate(reduced, axis=1)

    change = dot32(attended, full_output)
    updated = from_windows(
        (shifted.astype(jnp.float32) + change).astype(jnp.bfloat16), height, width, WIN
    )
    moved = from_behind(updated[:, width - shift :], "lon", 1)
    atmosphere_out = jnp.concatenate([moved, updated[:, : width - shift]], axis=1)
    flux = dot32(atmosphere_out.reshape(tokens, model), flux_weight).astype(jnp.bfloat16)
    pieces = jnp.einsum("cf,kcd->kfd", flux, blocks, preferred_element_type=jnp.float32)
    fluxes = flux_weight.shape[1]
    every = small_gather(pieces.reshape(2 * fluxes, tokens), devices, 2)
    every = every.reshape(devices, 2, fluxes, tokens)
    here = (regrid_target == position)[:, :, None, None]
    arrived = jnp.sum(jnp.where(here, every, 0.0), axis=(0, 1))
    forcing = jnp.dot(arrived.T, flux_embed, precision=HIGHEST).reshape(height, width, channels)
    forced = (ocean_state.astype(jnp.float32) + forcing).astype(jnp.bfloat16)
    reach = KERNEL // 2
    margin = extended(forced, (("lon", 1),), reach)
    padded = jnp.pad(margin.astype(jnp.float32), ((reach, reach), (0, 0), (0, 0)))
    conv = depthwise_conv(padded, depthwise, height, width)
    ocean_normed = layer_norm(conv, ocean_gain).astype(jnp.bfloat16)
    hidden = jax.nn.gelu(dot32(ocean_normed.reshape(tokens, channels), expand)).astype(jnp.bfloat16)
    ocean_change = dot32(hidden, contract).reshape(height, width, channels)
    ocean_next = (
        ocean_state.astype(jnp.float32) + ocean_mask.astype(jnp.float32)[..., None] * ocean_change
    ).astype(jnp.bfloat16)
    return (atmosphere_out, ocean_next, weight_grad)


def solution(mesh):
    return jax.shard_map(
        per_device,
        mesh=mesh,
        in_specs=(
            P("groups", "lon", None),
            P("groups", "lon", None),
            P("groups", "lon", None),
            P("groups", "lon"),
            P("lon", None),
            P("lon", None),
            P(),
            P(),
            P(),
            P(),
            P(),
            P(),
            P(),
            P(),
            P(),
            P("lon", None, None, None),
            P(),
        ),
        out_specs=(P("groups", "lon", None), P("groups", "lon", None), P(("groups", "lon"), None)),
        check_vma=False,
    )
```

```python
import functools

import jax
import jax.numpy as jnp
from jax import lax
from jax.experimental import pallas as pl
from jax.experimental.pallas import tpu as pltpu
from jax.sharding import PartitionSpec as P

HEAD_DIM = 32
WIN = 8
KERNEL = 7
LANES = 4
PACK = 4


EPSILON = 1e-05
HIGHEST = lax.Precision.HIGHEST
MESH = pl.DeviceIdType.MESH


def from_behind(block, axis, distance):
    devices = range(lax.axis_size(axis))
    route = [((i - distance) % len(devices), i) for i in devices]
    return lax.ppermute(block, axis, route)


def extended(shard, sides, width):
    for axis, dim in sides:
        peers, length = (lax.axis_size(axis), shard.shape[dim])
        up = [(i, (i + 1) % peers) for i in range(peers)]
        down = [(j, i) for i, j in up]
        last = lax.slice_in_dim(shard, length - width, length, axis=dim)
        leading = lax.slice_in_dim(shard, 0, width, axis=dim)
        before = lax.ppermute(last, axis, up)
        after = lax.ppermute(leading, axis, down)
        shard = jnp.concatenate([before, shard, after], axis=dim)
    return shard


def layer_norm(values, gain):
    center = values - jnp.mean(values, axis=-1, keepdims=True)
    spread = jnp.mean(center * center, axis=-1, keepdims=True)
    return center * lax.rsqrt(spread + EPSILON) * gain


def to_windows(values, window):
    height, width, depth = values.shape
    blocks = values.reshape(height // window, window, width // window, window, depth)
    return blocks.transpose(0, 2, 1, 3, 4).reshape(-1, depth)


def from_windows(values, height, width, window):
    depth = values.shape[-1]
    blocks = values.reshape(height // window, width // window, window, window, depth)
    return blocks.transpose(0, 2, 1, 3, 4).reshape(height, width, depth)


def ring_place(chip, chips):
    if chips != 8:
        return chip
    return (chip % 2) * (chips - 1 - chip // 2) + (1 - chip % 2) * (chip // 2)


def ring_chip(place, chips):
    if chips != 8:
        return place
    back = place // (chips // 2)
    return (1 - back) * (2 * place) + back * (2 * (chips - 1 - place) + 1)


def meet_all(n, me):
    barrier = pltpu.get_barrier_semaphore()

    def greet(offset, carry):
        pl.semaphore_signal(
            barrier, inc=1, device_id={"lon": (me + offset) % n}, device_id_type=MESH
        )
        return carry

    lax.fori_loop(1, n, greet, 0)
    pl.semaphore_wait(barrier, n - 1)


def direct_copy(src, dst, sems, offset, peer):
    return pltpu.make_async_remote_copy(
        src_ref=src,
        dst_ref=dst,
        send_sem=sems.at[0, offset],
        recv_sem=sems.at[1, offset],
        device_id={"lon": peer},
        device_id_type=MESH,
    )


def small_gather_kernel(n, x_ref, out_ref, sems):
    me = lax.axis_index("lon")
    meet_all(n, me)

    def send(offset, carry):
        direct_copy(x_ref, out_ref.at[me], sems, offset, (me + offset) % n).start()
        return carry

    def wait(offset, carry):
        copy = direct_copy(x_ref, out_ref.at[(me + n - offset) % n], sems, offset, (me + offset) % n)
        copy.wait()
        return carry

    lax.fori_loop(1, n, send, 0)
    out_ref[me] = x_ref[...]
    lax.fori_loop(1, n, wait, 0)


def small_gather(x, n, collective_id):
    return pl.pallas_call(
        functools.partial(small_gather_kernel, n),
        out_shape=jax.ShapeDtypeStruct((n,) + x.shape, x.dtype),
        in_specs=[pl.BlockSpec(memory_space=pltpu.VMEM)],
        out_specs=pl.BlockSpec(memory_space=pltpu.VMEM),
        scratch_shapes=[pltpu.SemaphoreType.DMA((2, n))],
        compiler_params=pltpu.CompilerParams(collective_id=collective_id, has_side_effects=True),
    )(x)


def gather_weights_kernel(
    n, proj_ref, out_weight_ref, surface_ref, w_ref, s_ref, ring_sems, pair_sems, own_sems, near_sems
):
    rows, width = out_weight_ref.shape
    chips = n // 2
    me = lax.axis_index("lon")
    core = me % 2
    place = ring_place(me // 2, chips)
    sibling = me + 1 - 2 * core

    own = []
    for lane in range(LANES):
        src = proj_ref.at[:, pl.ds(lane * width, width)] if lane < LANES - 1 else out_weight_ref
        own.append(
            pltpu.make_async_copy(
                src, w_ref.at[pl.ds(me * rows, rows), pl.ds(lane * width, width)], own_sems.at[lane]
            )
        )
        own[-1].start()
    own.append(pltpu.make_async_copy(surface_ref, s_ref.at[me], own_sems.at[LANES]))
    own[-1].start()
    meet_all(n, me)

    def send_near(offset, carry):
        direct_copy(surface_ref, s_ref.at[me], near_sems, offset, (me + offset) % n).start()
        return carry

    def wait_near(offset, carry):
        direct_copy(
            surface_ref, s_ref.at[(me + n - offset) % n], near_sems, offset, (me + offset) % n
        ).wait()
        return carry

    def slot(lane, distance, half):
        owner = ring_chip((place + distance) % chips, chips) * 2 + half
        return w_ref.at[
            pl.ds(pl.multiple_of(owner * rows, rows), rows), pl.ds(lane * width, width)
        ]

    def behind(lane, step):
        return step if lane % 2 else chips - step

    def ring_copy(lane, step, distance):
        ahead = chips - 1 if lane % 2 else 1
        block = slot(lane, distance, core)
        return pltpu.make_async_remote_copy(
            src_ref=block,
            dst_ref=block,
            send_sem=ring_sems.at[0, lane, step],
            recv_sem=ring_sems.at[1, lane, step],
            device_id={"lon": ring_chip((place + ahead) % chips, chips) * 2 + core},
            device_id_type=MESH,
        )

    def pair_copy(lane, step, half):
        block = slot(lane, behind(lane, step), half)
        return pltpu.make_async_remote_copy(
            src_ref=block,
            dst_ref=block,
            send_sem=pair_sems.at[0, lane, step],
            recv_sem=pair_sems.at[1, lane, step],
            device_id={"lon": sibling},
            device_id_type=MESH,
        )

    for copy in own:
        copy.wait()
    for lane in range(LANES):
        ring_copy(lane, 0, behind(lane, 0)).start()
    lax.fori_loop(1, n, send_near, 0)
    for lane in range(LANES):
        pair_copy(lane, 0, core).start()

    def step_on(step, carry):
        for lane in range(LANES):
            ring_copy(lane, step - 1, behind(lane, step)).wait_recv()
            ring_copy(lane, step, behind(lane, step)).start()
            pair_copy(lane, step, core).start()
        return carry

    lax.fori_loop(1, chips - 1, step_on, 0)
    for lane in range(LANES):
        ring_copy(lane, chips - 2, behind(lane, chips - 1)).wait_recv()
        pair_copy(lane, chips - 1, core).start()

    def drain(step, carry):
        for lane in range(LANES):
            ring_copy(lane, step, behind(lane, step)).wait_send()
        return carry

    def drain_pair(step, carry):
        for lane in range(LANES):
            pair_copy(lane, step, core).wait_send()
            pair_copy(lane, step, 1 - core).wait_recv()
        return carry

    lax.fori_loop(1, n, wait_near, 0)
    lax.fori_loop(0, chips - 1, drain, 0)
    lax.fori_loop(0, chips, drain_pair, 0)


def gather_weights(projection, output_weight, surface, n):
    rows, width = output_weight.shape
    chips = n // 2
    anywhere = pl.BlockSpec(memory_space=pl.ANY)
    return pl.pallas_call(
        functools.partial(gather_weights_kernel, n),
        out_shape=(
            jax.ShapeDtypeStruct((n * rows, LANES * width), projection.dtype),
            jax.ShapeDtypeStruct((n,) + surface.shape, surface.dtype),
        ),
        in_specs=[anywhere] * 3,
        out_specs=(anywhere, anywhere),
        scratch_shapes=[
            pltpu.SemaphoreType.DMA((2, LANES, chips - 1)),
            pltpu.SemaphoreType.DMA((2, LANES, chips)),
            pltpu.SemaphoreType.DMA((LANES + 1,)),
            pltpu.SemaphoreType.DMA((2, n)),
        ],
        compiler_params=pltpu.CompilerParams(collective_id=0, has_side_effects=True),
    )(projection, output_weight, surface)


def attention_kernel(packed_ref, grad_ref, attended_ref, grad_packed_ref):
    tokens, model = grad_ref.shape
    lanes = PACK * HEAD_DIM
    spread = PACK * tokens
    row_head = lax.broadcasted_iota(jnp.int32, (spread, lanes), 0) // tokens
    column_head = lax.broadcasted_iota(jnp.int32, (spread, lanes), 1) // HEAD_DIM
    own_head = row_head == column_head
    head_of = lax.broadcasted_iota(jnp.int32, (tokens, lanes), 1) // HEAD_DIM
    lower = lax.broadcasted_iota(jnp.int32, (tokens, 2 * tokens), 1) < tokens

    def expand_heads(block):
        tiled = jnp.concatenate([block] * PACK, axis=0)
        return jnp.where(own_head, tiled, jnp.zeros_like(tiled))

    def collapse_heads(block):
        total = jnp.where(head_of == 0, block[:tokens], 0.0)
        for head in range(1, PACK):
            total = total + jnp.where(head_of == head, block[head * tokens : (head + 1) * tokens], 0.0)
        return total

    def per_head(values, reduce, neutral):
        parts = []
        for start in range(0, spread, 2 * tokens):
            part = values[:, start : start + 2 * tokens]
            low = reduce(jnp.where(lower, part, neutral), axis=1, keepdims=True)
            high = reduce(jnp.where(lower, neutral, part), axis=1, keepdims=True)
            parts.append(jnp.where(lower, low, high))
        return jnp.concatenate(parts, axis=1)

    def product(left, right, contract):
        return lax.dot_general(
            left, right, (contract, ((), ())), preferred_element_type=jnp.float32
        )

    last, first = ((1,), (1,)), ((0,), (0,))
    plain = ((1,), (0,))
    scale = HEAD_DIM ** (-0.5)
    for group in range(model // lanes):
        at = group * lanes
        query = packed_ref[:, at : at + lanes]
        keys = expand_heads(packed_ref[:, model + at : model + at + lanes])
        values = expand_heads(packed_ref[:, 2 * model + at : 2 * model + at + lanes])
        grad = grad_ref[:, at : at + lanes]
        scores = product(query, keys, last) * scale
        powers = jnp.exp(scores - per_head(scores, jnp.max, -jnp.inf))
        probs = powers / per_head(powers, jnp.sum, 0.0)
        weights = probs.astype(jnp.bfloat16)
        attended_ref[:, at : at + lanes] = product(weights, values, plain).astype(jnp.bfloat16)
        grad_probs = product(grad, values, last)
        grad_values = collapse_heads(product(weights, grad, first))
        inner = per_head(grad_probs * probs, jnp.sum, 0.0)
        grad_scores = (probs * (grad_probs - inner) * scale).astype(jnp.bfloat16)
        grad_query = product(grad_scores, keys, plain)
        grad_keys = collapse_heads(product(grad_scores, query, first))
        grad_packed_ref[:, at : at + lanes] = grad_query.astype(jnp.bfloat16)
        grad_packed_ref[:, model + at : model + at + lanes] = grad_keys.astype(jnp.bfloat16)
        grad_packed_ref[:, 2 * model + at : 2 * model + at + lanes] = grad_values.astype(jnp.bfloat16)


def attention(packed, grad_att):
    tokens, model = grad_att.shape
    cells = WIN * WIN
    wide = pl.BlockSpec((cells, 3 * model), lambda w: (w, 0))
    narrow = pl.BlockSpec((cells, model), lambda w: (w, 0))
    return pl.pallas_call(
        attention_kernel,
        grid=(tokens // cells,),
        out_shape=(
            jax.ShapeDtypeStruct((tokens, model), jnp.bfloat16),
            jax.ShapeDtypeStruct((tokens, 3 * model), jnp.bfloat16),
        ),
        in_specs=[wide, narrow],
        out_specs=(narrow, wide),
        compiler_params=pltpu.CompilerParams(vmem_limit_bytes=48 * 1024 * 1024),
        cost_estimate=pl.CostEstimate(
            flops=14 * tokens * cells * model * PACK,
            bytes_accessed=16 * tokens * model,
            transcendentals=tokens * cells * (model // HEAD_DIM),
        ),
    )(packed, grad_att)


def depthwise_conv(padded, kernel, height, width):
    reach = kernel.shape[0]
    total = jnp.zeros((height, width, kernel.shape[2]), jnp.float32)
    for row in range(reach):
        for column in range(reach):
            total = (
                total + padded[row : row + height, column : column + width] * kernel[row, column]
            )
    return total


def dot32(left, right):
    return jnp.dot(left, right, preferred_element_type=jnp.float32)


def largest(values):
    return jnp.max(jnp.abs(values)).astype(jnp.float32)


class Ring:
    def __init__(self, terms, scale, forward, devices, position):
        self.chips = devices // 2
        self.terms, self.scale = terms, scale
        self.place = ring_place(position // 2, self.chips)
        self.ahead = 1 if forward else -1
        self.route = []
        for device in range(devices):
            peer = ring_chip(
                (ring_place(device // 2, self.chips) + self.ahead) % self.chips, self.chips
            )
            self.route.append((device, peer * 2 + device % 2))

    def term(self, distance):
        chip = ring_chip(
            (self.place + self.ahead * distance + 2 * self.chips) % self.chips, self.chips
        )
        return lax.dynamic_index_in_dim(self.terms, chip, 0, keepdims=False) * self.scale

    def first(self):
        return self.term(-1).astype(jnp.float16)

    def step(self, moving, step):
        moving = lax.ppermute(moving, "lon", self.route).astype(jnp.float32)
        moving = moving + self.term(-2 - step)
        return moving.astype(jnp.float16) if step < self.chips - 2 else moving / self.scale


def rings_beside(rings, stages, value):
    moving = [ring.first() for ring in rings]
    steps = rings[0].chips - 1
    for step in range(max(steps, len(stages))):
        moving, value = lax.optimization_barrier((moving, value))
        if step < steps:
            moving = [ring.step(block, step) for ring, block in zip(rings, moving)]
        if step < len(stages):
            value = stages[step](value)
    return moving, value


def per_device(
    atmosphere,
    cotangent,
    ocean_state,
    ocean_mask,
    projection,
    output_weight,
    attention_gain,
    surface_embed,
    surface_read,
    flux_weight,
    flux_embed,
    depthwise,
    ocean_gain,
    expand,
    contract,
    regrid_blocks,
    regrid_target,
):
    height, width, model = atmosphere.shape
    channels = ocean_state.shape[2]
    shift = WIN // 2
    tokens = height * width
    devices = lax.axis_size("lon")
    position = lax.axis_index("lon")
    chips = devices // 2
    core = position % 2
    blocks = regrid_blocks[0]
    targets = lax.dynamic_index_in_dim(regrid_target, position, 0, keepdims=False)
    surface = dot32(ocean_state.reshape(tokens, channels), surface_read).astype(jnp.bfloat16)
    all_weights, surfaces = gather_weights(
        projection,
        output_weight,
        jnp.broadcast_to(surface.astype(jnp.float32)[None], (8, tokens)),
        devices,
    )
    picked = jnp.take(surfaces[:, 0], targets, axis=0).astype(jnp.bfloat16)
    lifted = jnp.einsum("kcd,kd->c", blocks, picked, preferred_element_type=jnp.float32)
    state = (
        atmosphere.astype(jnp.float32) + lifted.reshape(height, width)[..., None] * surface_embed
    ).astype(jnp.bfloat16)
    full_projection, full_output = all_weights[:, : 3 * model], all_weights[:, 3 * model :]
    edges = (
        from_behind(state[:, :shift], "lon", -1),
        from_behind(cotangent[:, :shift], "lon", -1),
    )
    shifted = to_windows(jnp.concatenate([state[:, shift:], edges[0]], axis=1), WIN)
    grad_flat = to_windows(jnp.concatenate([cotangent[:, shift:], edges[1]], axis=1), WIN)
    normed = layer_norm(shifted.astype(jnp.float32), attention_gain).astype(jnp.bfloat16)
    packed = dot32(normed, full_projection).astype(jnp.bfloat16)
    grad_att = lax.dot_general(
        grad_flat, full_output, (((1,), (1,)), ((), ())), preferred_element_type=jnp.float32
    ).astype(jnp.bfloat16)
    attended, grad_packed = attention(packed, grad_att)

    bound = tokens * jnp.maximum(
        largest(normed) * largest(grad_packed), largest(attended) * largest(grad_flat)
    )
    bounds = small_gather(jnp.full((8, 128), bound, jnp.float32), devices, 1)
    scale = 30000.0 / jnp.maximum(jnp.sum(bounds[:, 0, 0]), 1e-30)

    pairs = [(i, i + 1 - 2 * (i % 2)) for i in range(devices)]

    def split_rows(values):
        turned = values.T.reshape(chips, 2, model // devices, tokens)
        mine = lax.dynamic_index_in_dim(turned, core, 1, keepdims=False)
        other = lax.dynamic_index_in_dim(turned, 1 - core, 1, keepdims=False)
        mine, other = (part.reshape(model // 2, tokens) for part in (mine, other))
        return mine, lax.ppermute(other, "lon", pairs)

    normed_rows = split_rows(normed)
    attended_rows = split_rows(attended)
    rights = [grad_packed[:, i * model : (i + 1) * model] for i in range(3)] + [grad_flat]
    rings = []
    for lane, right in enumerate(rights):
        rows = normed_rows if lane < 3 else attended_rows
        far = lax.ppermute(right, "lon", pairs)
        terms = (dot32(rows[0], right) + dot32(rows[1], far)).reshape(chips, -1, model)
        rings.append(Ring(terms, scale, lane % 2 == 0, devices, position))

    fluxes = flux_weight.shape[1]
    reach = KERNEL // 2

    def update(values):
        attended, shifted = values
        change = dot32(attended, full_output)
        updated = from_windows(
            (shifted.astype(jnp.float32) + change).astype(jnp.bfloat16), height, width, WIN
        )
        moved = from_behind(updated[:, width - shift :], "lon", 1)
        return jnp.concatenate([moved, updated[:, : width - shift]], axis=1)

    def regrid(atmosphere_out):
        flux = dot32(atmosphere_out.reshape(tokens, model), flux_weight).astype(jnp.bfloat16)
        pieces = jnp.einsum("cf,kcd->kfd", flux, blocks, preferred_element_type=jnp.float32)
        return atmosphere_out, pieces.reshape(2 * fluxes, tokens)

    def force(values):
        atmosphere_out, pieces = values
        every = small_gather(pieces, devices, 2).reshape(devices, 2, fluxes, tokens)
        here = (regrid_target == position)[:, :, None, None]
        arrived = jnp.sum(jnp.where(here, every, 0.0), axis=(0, 1))
        forcing = jnp.dot(arrived.T, flux_embed, precision=HIGHEST).reshape(
            height, width, channels
        )
        return atmosphere_out, (ocean_state.astype(jnp.float32) + forcing).astype(jnp.bfloat16)

    def convolve(values):
        atmosphere_out, forced = values
        margin = extended(forced, (("lon", 1),), reach)
        padded = jnp.pad(margin.astype(jnp.float32), ((reach, reach), (0, 0), (0, 0)))
        conv = depthwise_conv(padded, depthwise, height, width)
        ocean_normed = layer_norm(conv, ocean_gain).astype(jnp.bfloat16)
        return atmosphere_out, ocean_normed.reshape(tokens, channels)

    def advance(values):
        atmosphere_out, ocean_normed = values
        hidden = jax.nn.gelu(dot32(ocean_normed, expand)).astype(jnp.bfloat16)
        ocean_change = dot32(hidden, contract).reshape(height, width, channels)
        ocean_next = (
            ocean_state.astype(jnp.float32)
            + ocean_mask.astype(jnp.float32)[..., None] * ocean_change
        ).astype(jnp.bfloat16)
        return atmosphere_out, ocean_next

    reduced, (atmosphere_out, ocean_next) = rings_beside(
        rings, (update, regrid, force, convolve, advance), (attended, shifted)
    )
    weight_grad = jnp.concatenate(reduced, axis=1)
    return (atmosphere_out, ocean_next, weight_grad)


def solution(mesh):
    return jax.shard_map(
        per_device,
        mesh=mesh,
        in_specs=(
            P("groups", "lon", None),
            P("groups", "lon", None),
            P("groups", "lon", None),
            P("groups", "lon"),
            P("lon", None),
            P("lon", None),
            P(),
            P(),
            P(),
            P(),
            P(),
            P(),
            P(),
            P(),
            P(),
            P("lon", None, None, None),
            P(),
        ),
        out_specs=(P("groups", "lon", None), P("groups", "lon", None), P(("groups", "lon"), None)),
        check_vma=False,
    )
```

```python
import functools

import jax
import jax.numpy as jnp
from jax import lax
from jax.experimental import pallas as pl
from jax.experimental.pallas import tpu as pltpu
from jax.sharding import PartitionSpec as P

HEAD_DIM = 32
WIN = 8
KERNEL = 7
LANES = 4
PACK = 4


EPSILON = 1e-05
HIGHEST = lax.Precision.HIGHEST
MESH = pl.DeviceIdType.MESH


def from_behind(block, axis, distance):
    devices = range(lax.axis_size(axis))
    route = [((i - distance) % len(devices), i) for i in devices]
    return lax.ppermute(block, axis, route)


def extended(shard, sides, width):
    for axis, dim in sides:
        peers, length = (lax.axis_size(axis), shard.shape[dim])
        up = [(i, (i + 1) % peers) for i in range(peers)]
        down = [(j, i) for i, j in up]
        last = lax.slice_in_dim(shard, length - width, length, axis=dim)
        leading = lax.slice_in_dim(shard, 0, width, axis=dim)
        before = lax.ppermute(last, axis, up)
        after = lax.ppermute(leading, axis, down)
        shard = jnp.concatenate([before, shard, after], axis=dim)
    return shard


def layer_norm(values, gain):
    center = values - jnp.mean(values, axis=-1, keepdims=True)
    spread = jnp.mean(center * center, axis=-1, keepdims=True)
    return center * lax.rsqrt(spread + EPSILON) * gain


def to_windows(values, window):
    height, width, depth = values.shape
    blocks = values.reshape(height // window, window, width // window, window, depth)
    return blocks.transpose(0, 2, 1, 3, 4).reshape(-1, depth)


def from_windows(values, height, width, window):
    depth = values.shape[-1]
    blocks = values.reshape(height // window, width // window, window, window, depth)
    return blocks.transpose(0, 2, 1, 3, 4).reshape(height, width, depth)


def ring_place(chip, chips):
    if chips != 8:
        return chip
    return (chip % 2) * (chips - 1 - chip // 2) + (1 - chip % 2) * (chip // 2)


def ring_chip(place, chips):
    if chips != 8:
        return place
    back = place // (chips // 2)
    return (1 - back) * (2 * place) + back * (2 * (chips - 1 - place) + 1)


def meet_all(n, me):
    barrier = pltpu.get_barrier_semaphore()

    def greet(offset, carry):
        pl.semaphore_signal(
            barrier, inc=1, device_id={"lon": (me + offset) % n}, device_id_type=MESH
        )
        return carry

    lax.fori_loop(1, n, greet, 0)
    pl.semaphore_wait(barrier, n - 1)


def direct_copy(src, dst, sems, offset, peer):
    return pltpu.make_async_remote_copy(
        src_ref=src,
        dst_ref=dst,
        send_sem=sems.at[0, offset],
        recv_sem=sems.at[1, offset],
        device_id={"lon": peer},
        device_id_type=MESH,
    )


def small_gather_kernel(n, x_ref, out_ref, sems):
    me = lax.axis_index("lon")
    meet_all(n, me)

    def send(offset, carry):
        direct_copy(x_ref, out_ref.at[me], sems, offset, (me + offset) % n).start()
        return carry

    def wait(offset, carry):
        copy = direct_copy(x_ref, out_ref.at[(me + n - offset) % n], sems, offset, (me + offset) % n)
        copy.wait()
        return carry

    lax.fori_loop(1, n, send, 0)
    out_ref[me] = x_ref[...]
    lax.fori_loop(1, n, wait, 0)


def small_gather(x, n, collective_id):
    return pl.pallas_call(
        functools.partial(small_gather_kernel, n),
        out_shape=jax.ShapeDtypeStruct((n,) + x.shape, x.dtype),
        in_specs=[pl.BlockSpec(memory_space=pltpu.VMEM)],
        out_specs=pl.BlockSpec(memory_space=pltpu.VMEM),
        scratch_shapes=[pltpu.SemaphoreType.DMA((2, n))],
        compiler_params=pltpu.CompilerParams(collective_id=collective_id, has_side_effects=True),
    )(x)


def gather_weights_kernel(
    n, proj_ref, out_weight_ref, surface_ref, w_ref, s_ref, ring_sems, pair_sems, own_sems, near_sems
):
    rows, width = out_weight_ref.shape
    chips = n // 2
    me = lax.axis_index("lon")
    core = me % 2
    place = ring_place(me // 2, chips)
    sibling = me + 1 - 2 * core

    own = []
    for lane in range(LANES):
        src = proj_ref.at[:, pl.ds(lane * width, width)] if lane < LANES - 1 else out_weight_ref
        own.append(
            pltpu.make_async_copy(
                src, w_ref.at[pl.ds(me * rows, rows), pl.ds(lane * width, width)], own_sems.at[lane]
            )
        )
        own[-1].start()
    own.append(pltpu.make_async_copy(surface_ref, s_ref.at[me], own_sems.at[LANES]))
    own[-1].start()
    meet_all(n, me)

    def send_near(offset, carry):
        direct_copy(surface_ref, s_ref.at[me], near_sems, offset, (me + offset) % n).start()
        return carry

    def wait_near(offset, carry):
        direct_copy(
            surface_ref, s_ref.at[(me + n - offset) % n], near_sems, offset, (me + offset) % n
        ).wait()
        return carry

    def slot(lane, distance, half):
        owner = ring_chip((place + distance) % chips, chips) * 2 + half
        return w_ref.at[
            pl.ds(pl.multiple_of(owner * rows, rows), rows), pl.ds(lane * width, width)
        ]

    def behind(lane, step):
        return step if lane % 2 else chips - step

    def ring_copy(lane, step, distance):
        ahead = chips - 1 if lane % 2 else 1
        block = slot(lane, distance, core)
        return pltpu.make_async_remote_copy(
            src_ref=block,
            dst_ref=block,
            send_sem=ring_sems.at[0, lane, step],
            recv_sem=ring_sems.at[1, lane, step],
            device_id={"lon": ring_chip((place + ahead) % chips, chips) * 2 + core},
            device_id_type=MESH,
        )

    def pair_copy(lane, step, half):
        block = slot(lane, behind(lane, step), half)
        return pltpu.make_async_remote_copy(
            src_ref=block,
            dst_ref=block,
            send_sem=pair_sems.at[0, lane, step],
            recv_sem=pair_sems.at[1, lane, step],
            device_id={"lon": sibling},
            device_id_type=MESH,
        )

    for copy in own:
        copy.wait()
    for lane in range(LANES):
        ring_copy(lane, 0, behind(lane, 0)).start()
    lax.fori_loop(1, n, send_near, 0)
    for lane in range(LANES):
        pair_copy(lane, 0, core).start()

    def step_on(step, carry):
        for lane in range(LANES):
            ring_copy(lane, step - 1, behind(lane, step)).wait_recv()
            ring_copy(lane, step, behind(lane, step)).start()
            pair_copy(lane, step, core).start()
        return carry

    lax.fori_loop(1, chips - 1, step_on, 0)
    for lane in range(LANES):
        ring_copy(lane, chips - 2, behind(lane, chips - 1)).wait_recv()
        pair_copy(lane, chips - 1, core).start()

    def drain(step, carry):
        for lane in range(LANES):
            ring_copy(lane, step, behind(lane, step)).wait_send()
        return carry

    def drain_pair(step, carry):
        for lane in range(LANES):
            pair_copy(lane, step, core).wait_send()
            pair_copy(lane, step, 1 - core).wait_recv()
        return carry

    lax.fori_loop(1, n, wait_near, 0)
    lax.fori_loop(0, chips - 1, drain, 0)
    lax.fori_loop(0, chips, drain_pair, 0)


def gather_weights(projection, output_weight, surface, n):
    rows, width = output_weight.shape
    chips = n // 2
    anywhere = pl.BlockSpec(memory_space=pl.ANY)
    return pl.pallas_call(
        functools.partial(gather_weights_kernel, n),
        out_shape=(
            jax.ShapeDtypeStruct((n * rows, LANES * width), projection.dtype),
            jax.ShapeDtypeStruct((n,) + surface.shape, surface.dtype),
        ),
        in_specs=[anywhere] * 3,
        out_specs=(anywhere, anywhere),
        scratch_shapes=[
            pltpu.SemaphoreType.DMA((2, LANES, chips - 1)),
            pltpu.SemaphoreType.DMA((2, LANES, chips)),
            pltpu.SemaphoreType.DMA((LANES + 1,)),
            pltpu.SemaphoreType.DMA((2, n)),
        ],
        compiler_params=pltpu.CompilerParams(collective_id=0, has_side_effects=True),
    )(projection, output_weight, surface)


def attention_kernel(packed_ref, grad_ref, attended_ref, grad_packed_ref):
    tokens, model = grad_ref.shape
    lanes = PACK * HEAD_DIM
    spread = PACK * tokens
    row_head = lax.broadcasted_iota(jnp.int32, (spread, lanes), 0) // tokens
    column_head = lax.broadcasted_iota(jnp.int32, (spread, lanes), 1) // HEAD_DIM
    own_head = row_head == column_head
    head_of = lax.broadcasted_iota(jnp.int32, (tokens, lanes), 1) // HEAD_DIM
    lower = lax.broadcasted_iota(jnp.int32, (tokens, 2 * tokens), 1) < tokens

    def expand_heads(block):
        tiled = jnp.concatenate([block] * PACK, axis=0)
        return jnp.where(own_head, tiled, jnp.zeros_like(tiled))

    def collapse_heads(block):
        total = jnp.where(head_of == 0, block[:tokens], 0.0)
        for head in range(1, PACK):
            total = total + jnp.where(head_of == head, block[head * tokens : (head + 1) * tokens], 0.0)
        return total

    def per_head(values, reduce, neutral):
        parts = []
        for start in range(0, spread, 2 * tokens):
            part = values[:, start : start + 2 * tokens]
            low = reduce(jnp.where(lower, part, neutral), axis=1, keepdims=True)
            high = reduce(jnp.where(lower, neutral, part), axis=1, keepdims=True)
            parts.append(jnp.where(lower, low, high))
        return jnp.concatenate(parts, axis=1)

    def product(left, right, contract):
        return lax.dot_general(
            left, right, (contract, ((), ())), preferred_element_type=jnp.float32
        )

    last, first = ((1,), (1,)), ((0,), (0,))
    plain = ((1,), (0,))
    scale = HEAD_DIM ** (-0.5)
    for group in range(model // lanes):
        at = group * lanes
        query = packed_ref[:, at : at + lanes]
        keys = expand_heads(packed_ref[:, model + at : model + at + lanes])
        values = expand_heads(packed_ref[:, 2 * model + at : 2 * model + at + lanes])
        grad = grad_ref[:, at : at + lanes]
        scores = product(query, keys, last) * scale
        powers = jnp.exp(scores - per_head(scores, jnp.max, -jnp.inf))
        probs = powers / per_head(powers, jnp.sum, 0.0)
        weights = probs.astype(jnp.bfloat16)
        attended_ref[:, at : at + lanes] = product(weights, values, plain).astype(jnp.bfloat16)
        grad_probs = product(grad, values, last)
        grad_values = collapse_heads(product(weights, grad, first))
        inner = per_head(grad_probs * probs, jnp.sum, 0.0)
        grad_scores = (probs * (grad_probs - inner) * scale).astype(jnp.bfloat16)
        grad_query = product(grad_scores, keys, plain)
        grad_keys = collapse_heads(product(grad_scores, query, first))
        grad_packed_ref[:, at : at + lanes] = grad_query.astype(jnp.bfloat16)
        grad_packed_ref[:, model + at : model + at + lanes] = grad_keys.astype(jnp.bfloat16)
        grad_packed_ref[:, 2 * model + at : 2 * model + at + lanes] = grad_values.astype(jnp.bfloat16)


def attention(packed, grad_att):
    tokens, model = grad_att.shape
    cells = WIN * WIN
    wide = pl.BlockSpec((cells, 3 * model), lambda w: (w, 0))
    narrow = pl.BlockSpec((cells, model), lambda w: (w, 0))
    return pl.pallas_call(
        attention_kernel,
        grid=(tokens // cells,),
        out_shape=(
            jax.ShapeDtypeStruct((tokens, model), jnp.bfloat16),
            jax.ShapeDtypeStruct((tokens, 3 * model), jnp.bfloat16),
        ),
        in_specs=[wide, narrow],
        out_specs=(narrow, wide),
        compiler_params=pltpu.CompilerParams(vmem_limit_bytes=48 * 1024 * 1024),
        cost_estimate=pl.CostEstimate(
            flops=14 * tokens * cells * model * PACK,
            bytes_accessed=16 * tokens * model,
            transcendentals=tokens * cells * (model // HEAD_DIM),
        ),
    )(packed, grad_att)


def depthwise_conv(padded, kernel, height, width):
    reach = kernel.shape[0]
    total = jnp.zeros((height, width, kernel.shape[2]), jnp.float32)
    for row in range(reach):
        for column in range(reach):
            total = (
                total + padded[row : row + height, column : column + width] * kernel[row, column]
            )
    return total


def dot32(left, right):
    return jnp.dot(left, right, preferred_element_type=jnp.float32)


def largest(values):
    return jnp.max(jnp.abs(values)).astype(jnp.float32)


class Ring:
    def __init__(self, terms, scale, forward, devices, position):
        self.chips = devices // 2
        self.terms, self.scale = terms, scale
        self.place = ring_place(position // 2, self.chips)
        self.ahead = 1 if forward else -1
        self.route = []
        for device in range(devices):
            peer = ring_chip(
                (ring_place(device // 2, self.chips) + self.ahead) % self.chips, self.chips
            )
            self.route.append((device, peer * 2 + device % 2))

    def term(self, distance):
        chip = ring_chip(
            (self.place + self.ahead * distance + 2 * self.chips) % self.chips, self.chips
        )
        return lax.dynamic_index_in_dim(self.terms, chip, 0, keepdims=False) * self.scale

    def first(self):
        return self.term(-1).astype(jnp.float16)

    def step(self, moving, step):
        moving = lax.ppermute(moving, "lon", self.route).astype(jnp.float32)
        moving = moving + self.term(-2 - step)
        return moving.astype(jnp.float16) if step < self.chips - 2 else moving / self.scale


def rings_beside(rings, stages, value):
    moving = [ring.first() for ring in rings]
    steps = rings[0].chips - 1
    for step in range(max(steps, len(stages))):
        value = lax.optimization_barrier((moving, value))[1]
        if step < steps:
            moving = [ring.step(block, step) for ring, block in zip(rings, moving)]
        if step < len(stages):
            value = stages[step](value)
    return moving, value


def per_device(
    atmosphere,
    cotangent,
    ocean_state,
    ocean_mask,
    projection,
    output_weight,
    attention_gain,
    surface_embed,
    surface_read,
    flux_weight,
    flux_embed,
    depthwise,
    ocean_gain,
    expand,
    contract,
    regrid_blocks,
    regrid_target,
):
    height, width, model = atmosphere.shape
    channels = ocean_state.shape[2]
    shift = WIN // 2
    tokens = height * width
    devices = lax.axis_size("lon")
    position = lax.axis_index("lon")
    chips = devices // 2
    core = position % 2
    blocks = regrid_blocks[0]
    targets = lax.dynamic_index_in_dim(regrid_target, position, 0, keepdims=False)
    surface = dot32(ocean_state.reshape(tokens, channels), surface_read).astype(jnp.bfloat16)
    all_weights, surfaces = gather_weights(
        projection,
        output_weight,
        jnp.broadcast_to(surface.astype(jnp.float32)[None], (8, tokens)),
        devices,
    )
    picked = jnp.take(surfaces[:, 0], targets, axis=0).astype(jnp.bfloat16)
    lifted = jnp.einsum("kcd,kd->c", blocks, picked, preferred_element_type=jnp.float32)
    state = (
        atmosphere.astype(jnp.float32) + lifted.reshape(height, width)[..., None] * surface_embed
    ).astype(jnp.bfloat16)
    full_projection, full_output = all_weights[:, : 3 * model], all_weights[:, 3 * model :]
    edges = (
        from_behind(state[:, :shift], "lon", -1),
        from_behind(cotangent[:, :shift], "lon", -1),
    )
    shifted = to_windows(jnp.concatenate([state[:, shift:], edges[0]], axis=1), WIN)
    grad_flat = to_windows(jnp.concatenate([cotangent[:, shift:], edges[1]], axis=1), WIN)
    normed = layer_norm(shifted.astype(jnp.float32), attention_gain).astype(jnp.bfloat16)
    packed = dot32(normed, full_projection).astype(jnp.bfloat16)
    grad_att = lax.dot_general(
        grad_flat, full_output, (((1,), (1,)), ((), ())), preferred_element_type=jnp.float32
    ).astype(jnp.bfloat16)
    attended, grad_packed = attention(packed, grad_att)

    bound = tokens * jnp.maximum(
        largest(normed) * largest(grad_packed), largest(attended) * largest(grad_flat)
    )
    bounds = small_gather(jnp.full((8, 128), bound, jnp.float32), devices, 1)
    scale = 30000.0 / jnp.maximum(jnp.sum(bounds[:, 0, 0]), 1e-30)

    pairs = [(i, i + 1 - 2 * (i % 2)) for i in range(devices)]

    def split_rows(values):
        turned = values.T.reshape(chips, 2, model // devices, tokens)
        mine = lax.dynamic_index_in_dim(turned, core, 1, keepdims=False)
        other = lax.dynamic_index_in_dim(turned, 1 - core, 1, keepdims=False)
        mine, other = (part.reshape(model // 2, tokens) for part in (mine, other))
        return mine, lax.ppermute(other, "lon", pairs)

    normed_rows = split_rows(normed)
    attended_rows = split_rows(attended)
    rights = [grad_packed[:, i * model : (i + 1) * model] for i in range(3)] + [grad_flat]
    rings = []
    for lane, right in enumerate(rights):
        rows = normed_rows if lane < 3 else attended_rows
        far = lax.ppermute(right, "lon", pairs)
        terms = (dot32(rows[0], right) + dot32(rows[1], far)).reshape(chips, -1, model)
        rings.append(Ring(terms, scale, lane % 2 == 0, devices, position))

    fluxes = flux_weight.shape[1]
    reach = KERNEL // 2

    def update(values):
        attended, shifted = values
        change = dot32(attended, full_output)
        updated = from_windows(
            (shifted.astype(jnp.float32) + change).astype(jnp.bfloat16), height, width, WIN
        )
        moved = from_behind(updated[:, width - shift :], "lon", 1)
        return jnp.concatenate([moved, updated[:, : width - shift]], axis=1)

    def regrid(atmosphere_out):
        flux = dot32(atmosphere_out.reshape(tokens, model), flux_weight).astype(jnp.bfloat16)
        pieces = jnp.einsum("cf,kcd->kfd", flux, blocks, preferred_element_type=jnp.float32)
        return atmosphere_out, pieces.reshape(2 * fluxes, tokens)

    def force(values):
        atmosphere_out, pieces = values
        every = small_gather(pieces, devices, 2).reshape(devices, 2, fluxes, tokens)
        here = (regrid_target == position)[:, :, None, None]
        arrived = jnp.sum(jnp.where(here, every, 0.0), axis=(0, 1))
        forcing = jnp.dot(arrived.T, flux_embed, precision=HIGHEST).reshape(
            height, width, channels
        )
        return atmosphere_out, (ocean_state.astype(jnp.float32) + forcing).astype(jnp.bfloat16)

    def convolve(values):
        atmosphere_out, forced = values
        margin = extended(forced, (("lon", 1),), reach)
        padded = jnp.pad(margin.astype(jnp.float32), ((reach, reach), (0, 0), (0, 0)))
        conv = depthwise_conv(padded, depthwise, height, width)
        ocean_normed = layer_norm(conv, ocean_gain).astype(jnp.bfloat16)
        return atmosphere_out, ocean_normed.reshape(tokens, channels)

    def advance(values):
        atmosphere_out, ocean_normed = values
        hidden = jax.nn.gelu(dot32(ocean_normed, expand)).astype(jnp.bfloat16)
        ocean_change = dot32(hidden, contract).reshape(height, width, channels)
        ocean_next = (
            ocean_state.astype(jnp.float32)
            + ocean_mask.astype(jnp.float32)[..., None] * ocean_change
        ).astype(jnp.bfloat16)
        return atmosphere_out, ocean_next

    reduced, (atmosphere_out, ocean_next) = rings_beside(
        rings, (update, regrid, force, convolve, advance), (attended, shifted)
    )
    weight_grad = jnp.concatenate(reduced, axis=1)
    return (atmosphere_out, ocean_next, weight_grad)


def solution(mesh):
    return jax.shard_map(
        per_device,
        mesh=mesh,
        in_specs=(
            P("groups", "lon", None),
            P("groups", "lon", None),
            P("groups", "lon", None),
            P("groups", "lon"),
            P("lon", None),
            P("lon", None),
            P(),
            P(),
            P(),
            P(),
            P(),
            P(),
            P(),
            P(),
            P(),
            P("lon", None, None, None),
            P(),
        ),
        out_specs=(P("groups", "lon", None), P("groups", "lon", None), P(("groups", "lon"), None)),
        check_vma=False,
    )
```
